1024 devices in a mesh: wide: 128 (over y_lo, z, x), narrow: 8 (over y_hi, core).
Axes of the slice: x: 8, y: 8 (y_hi: 4, y_lo: 2; y = y_hi * 2 + y_lo), z: 8, core: 2. Of those that a mesh axis runs over, the one named last changes fastest.
Arguments:
- right_side: float32 [8, 2048, 12, 128], P('narrow', 'wide'), may hold values from -160 to 160
- hop_blocks: bfloat16 [8, 2048, 9, 64, 128], P('narrow', 'wide'), may hold values from -2 to 6
- restriction: float32 [8, 2048, 64, 128], P('narrow', 'wide'), may hold values from -0.25 to 0.25
Outputs:
- solution_field: float32 [8, 2048, 12, 128], P('narrow', 'wide')
- coarse_residual: float32 [8, 512, 12, 128], P(None, 'wide')
The draws below stay inside these ranges and needn't reach their ends.
All inputs are finite; a program needn't handle non-finite values.
Results may differ from the reference program's by a relative error of at most 0.0053.
Values may be sent and summed in bfloat16 or wider, within the bound.
A program may use at most 32 MiB of HBM per device.

```python
import math
import jax
import jax.numpy as jnp
from jax import lax

DOF = 64
DOF3 = 64
RHS = 12
ITERS = 4
LX = 8
YLOC = 2
LY = 16
LZ = 16
NT = 8
XYZ = 2048
XYZ3 = 512


def draw_right_side(key, part):
    shape = (NT, XYZ, RHS, 2 * DOF)
    key_base, key_cols, key_rough, key_blocks = jax.random.split(key, 4)
    time_pos = lax.broadcasted_iota(jnp.float32, shape, 0) / NT
    site_pos = lax.broadcasted_iota(jnp.float32, shape, 1) / XYZ
    ramp = jnp.exp(math.log(3.0) * (time_pos + site_pos))
    columns = jnp.exp(jax.random.uniform(key_cols, (1, 1, RHS, 1), jnp.float32, 0.0, math.log(10.0)))
    block_count = XYZ // (LX * YLOC)
    owner = jnp.arange(XYZ, dtype=jnp.int32) // (LX * YLOC)
    block_scale = jnp.exp(jax.random.uniform(key_blocks, (NT, block_count, RHS), jnp.float32, -0.5 * math.log(3.0), 0.5 * math.log(3.0)))
    spread = jnp.take(block_scale, owner, axis=1)[..., None]
    rough = jax.random.uniform(key_rough, shape, jnp.float32, 0.5, 1.5)
    base = jnp.clip(jax.random.normal(key_base, shape, jnp.float32), -4.0, 4.0)
    return ramp * columns * spread * rough * base / 6.0


def draw_hop_blocks(key, part):
    shape = (NT, XYZ, 9, DOF, 2 * DOF)
    key_noise, key_diag, key_imag, key_level, key_scale, key_strength = jax.random.split(key, 6)
    sigma = 0.35 / math.sqrt(2.0 * DOF)
    block_count = XYZ // (LX * YLOC)
    owner = jnp.arange(XYZ, dtype=jnp.int32) // (LX * YLOC)
    draw_scale = jnp.exp(jax.random.uniform(key_scale, (), jnp.float32, math.log(0.8), math.log(1.25)))
    draw_strength = jnp.exp(jax.random.uniform(key_strength, (), jnp.float32, math.log(0.7), math.log(1.4)))
    diag_table = jnp.exp(jax.random.uniform(key_diag, (NT, block_count), jnp.float32, math.log(1.5), math.log(4.0)))
    imag_table = jax.random.uniform(key_imag, (NT, block_count), jnp.float32, -1.5, 1.5)
    level_table = jnp.exp(jax.random.uniform(key_level, (NT, block_count), jnp.float32, -0.5 * math.log(3.0), 0.5 * math.log(3.0)))
    diag_real = jnp.take(draw_scale * diag_table, owner, axis=1)[:, :, None, None, None]
    diag_imag = jnp.take(imag_table, owner, axis=1)[:, :, None, None, None]
    level = jnp.take(draw_strength * level_table, owner, axis=1)[:, :, None, None, None]
    noise = jnp.clip(jax.random.normal(key_noise, shape, jnp.float32) * sigma, -4.0 * sigma, 4.0 * sigma)
    direction = lax.broadcasted_iota(jnp.int32, shape, 2)
    row_index = lax.broadcasted_iota(jnp.int32, shape, 3)
    col_index = lax.broadcasted_iota(jnp.int32, shape, 4)
    real_diag = jnp.where((direction == 0) & (row_index == col_index), diag_real, 0.0)
    imag_diag = jnp.where((direction == 0) & (col_index == row_index + DOF), diag_imag, 0.0)
    return (noise * level + real_diag + imag_diag).astype(jnp.bfloat16)


def shard_levels(key, dims, shards, least, largest):
    gain = 1.0
    for axis_at, shards_of in shards:
        heights = jax.random.uniform(jax.random.fold_in(jax.random.fold_in(key, 6), axis_at), (shards_of,), jnp.float32, least / len(shards), largest / len(shards))
        gain = gain * jnp.repeat(jnp.exp(heights), dims[axis_at] // shards_of).reshape((-1,) + (1,) * (len(dims) - 1 - axis_at))
    return gain


def centred(rng, dims, deviation, bound, cuts=(), kind=jnp.bfloat16):
    array = jax.random.normal(rng, dims, jnp.float32) * deviation
    if len(cuts) > 0:
        array = shard_levels(rng, dims, cuts, -0.22, 0.18) * array
    return jnp.clip(array, min=-bound, max=bound).astype(kind)


def setup_inputs(seed: int = 0) -> dict:
    keys = jax.random.split(jax.random.key(seed), 4)
    right_side = draw_right_side(jax.random.fold_in(keys[3], 71), 0)
    hop_blocks = draw_hop_blocks(jax.random.fold_in(keys[3], 71), 0)
    restriction = centred(keys[2], (NT, XYZ, DOF3, 2 * DOF), (8 * DOF) ** -0.5, 0.25, ((0, 8), (1, 128)), jnp.float32)
    return {"right_side": right_side, "hop_blocks": hop_blocks, "restriction": restriction}


def complex_pair(vector):
    half = vector.shape[-1] // 2
    real_part = vector[..., :half]
    imag_part = vector[..., half:]
    first = jnp.concatenate([real_part, -imag_part], -1)
    second = jnp.concatenate([imag_part, real_part], -1)
    return first, second


def spatial_views(slab):
    lattice = slab.reshape(LZ, LY, LX, slab.shape[1], slab.shape[2])
    views = [lattice,
             jnp.roll(lattice, -1, 2), jnp.roll(lattice, 1, 2),
             jnp.roll(lattice, -1, 1), jnp.roll(lattice, 1, 1),
             jnp.roll(lattice, -1, 0), jnp.roll(lattice, 1, 0)]
    return [view.reshape(slab.shape) for view in views]


def operate(rounded, hop_blocks):
    def one_slice(tindex):
        here = lax.dynamic_index_in_dim(rounded, tindex, 0, keepdims=False)
        later = lax.dynamic_index_in_dim(rounded, (tindex + 1) % NT, 0, keepdims=False)
        earlier = lax.dynamic_index_in_dim(rounded, (tindex + NT - 1) % NT, 0, keepdims=False)
        blocks = lax.dynamic_index_in_dim(hop_blocks, tindex, 0, keepdims=False)
        views = spatial_views(here) + [later, earlier]
        total = jnp.zeros((here.shape[0], here.shape[1], DOF * 2), jnp.float32)
        for direction in range(9):
            first, second = complex_pair(views[direction])
            block = blocks[:, direction].astype(jnp.float32)
            out_re = jnp.einsum("sak,srk->sra", block, first.astype(jnp.float32))
            out_im = jnp.einsum("sak,srk->sra", block, second.astype(jnp.float32))
            total = total + jnp.concatenate([out_re, out_im], -1)
        return total
    return lax.map(one_slice, jnp.arange(NT, dtype=jnp.int32))


def cmul(alpha_re, alpha_im, vector):
    half = vector.shape[-1] // 2
    real_part = vector[..., :half]
    imag_part = vector[..., half:]
    are = alpha_re[:, None]
    aim = alpha_im[:, None]
    return jnp.concatenate([are * real_part - aim * imag_part, are * imag_part + aim * real_part], -1)


def reference(right_side, hop_blocks, restriction):
    solution_field = jnp.zeros_like(right_side)
    residual = right_side
    half = DOF
    for step in range(ITERS):
        rounded = residual.astype(jnp.bfloat16)
        image = operate(rounded, hop_blocks)
        inner_re = jnp.sum(image * residual, axis=(0, 1, 3))
        inner_im = jnp.sum(image[..., :half] * residual[..., half:] - image[..., half:] * residual[..., :half], axis=(0, 1, 3))
        power = jnp.sum(image * image, axis=(0, 1, 3))
        alpha_re = inner_re / power
        alpha_im = inner_im / power
        solution_field = solution_field + cmul(alpha_re, alpha_im, residual)
        residual = residual - cmul(alpha_re, alpha_im, image)
    first, second = complex_pair(residual)
    out_re = jnp.einsum("tsak,tsrk->tsra", restriction, first, precision=lax.Precision.HIGHEST)
    out_im = jnp.einsum("tsak,tsrk->tsra", restriction, second, precision=lax.Precision.HIGHEST)
    persite = jnp.concatenate([out_re, out_im], -1)
    grouped = persite.reshape(NT, LZ, LY // 2, 2, LX // 2, 2, RHS, 2 * DOF3)
    coarse_residual = jnp.sum(grouped, axis=(3, 5)).reshape(NT, XYZ3, RHS, 2 * DOF3)
    return solution_field, coarse_residual
```

```python
import jax
import jax.numpy as jnp
from jax import lax
from jax.experimental import pallas as pl
from jax.experimental.pallas import tpu as pltpu
from jax.sharding import PartitionSpec as P

F32, BF16 = jnp.float32, jnp.bfloat16
MESH = pl.DeviceIdType.MESH
ITERS = 4
RHS = 12
SITES = 16
HALF = 64
ROWS = SITES * RHS
SLAB = ROWS // 2
PACK = 4 * RHS
SCALE = 1.0 / 16.0


def dot(lhs, rhs):
    return lax.dot_general(lhs, rhs, (((1,), (1,)), ((), ())), preferred_element_type=F32)


def split(value):
    high = value.astype(BF16)
    return high, (value - high.astype(F32)).astype(BF16)


def paired(rows):
    lane = lax.broadcasted_iota(jnp.int32, rows.shape, 1)
    sign = jnp.where(lane < HALF, 1.0, -1.0).astype(rows.dtype)
    return jnp.concatenate([rows * sign, pltpu.roll(rows, HALF, 1)], 0)


def unpack(first, second):
    first = jnp.concatenate([first[0:24, 0:128], first[24:48, 128:256]], 0)
    second = jnp.concatenate([second[0:24, 0:128], second[24:48, 128:256]], 0)
    row = lax.broadcasted_iota(jnp.int32, (PACK, 128), 0)
    lane = lax.broadcasted_iota(jnp.int32, (PACK, 128), 1)
    even = (row < 12) | ((row >= 24) & (row < 36))
    moved = pltpu.roll(jnp.where(even, second, first), HALF, 1)
    return jnp.where(even == (lane < HALF), jnp.where(even, first, second), moved)


def body(
    right_ref, hop_ref, rest_ref, x_ref, coarse_ref,
    rin, hop, rest, vecs, sent, local, big, rows, acc, grams, message, slots0, slots1, slots2, wide_msg,
    rest_hi, rest_lo, mine, xout,
    load_sem, send_sem, recv_sem, red_send, red_recv, gat_send, gat_recv, out_sem,
):
    w = lax.axis_index("wide")
    n = lax.axis_index("narrow")
    ylat, zlat = w % 8, w // 8
    px, pz, plo = w % 8, (w // 8) % 8, w // 64
    phi, pc = n // 2, n % 2
    py = phi * 2 + plo

    load_right = pltpu.make_async_copy(right_ref, rin, load_sem.at[0])
    load_right.start()
    load_hop = pltpu.make_async_copy(hop_ref, hop, load_sem.at[1])
    load_hop.start()
    load_rest = pltpu.make_async_copy(rest_ref, rest, load_sem.at[2])
    load_rest.start()

    z_up, z_down = (((zlat + 1) % 16) * 8 + ylat, n), (((zlat + 15) % 16) * 8 + ylat, n)
    y_up, y_down = (zlat * 8 + (ylat + 1) % 8, n), (zlat * 8 + (ylat + 7) % 8, n)
    t_up, t_down = (w, (n + 1) % 8), (w, (n + 7) % 8)

    def at_x(dx, dc):
        return ((w // 8) * 8 + (px + dx) % 8, phi * 2 + (pc + dc) % 2)

    def at_z(dz):
        return (plo * 64 + ((pz + dz) % 8) * 8 + px, n)

    def at_y(dy):
        other = (py + dy) % 8
        return ((other % 2) * 64 + pz * 8 + px, (other // 2) * 2 + pc)

    phase0 = [at_x(dx, dc) for dx in range(8) for dc in range(2) if dx or dc]
    phase1 = [at_z(dz) for dz in range(1, 8)]
    phase2 = [at_y(dy) for dy in range(1, 8)]

    greeted = [z_up, z_down, t_up, t_down] + phase0 + phase1 + phase2
    barrier = pltpu.get_barrier_semaphore()
    for device in greeted:
        pl.semaphore_signal(barrier, inc=1, device_id=device, device_id_type=MESH)

    load_right.wait()
    for site in range(SITES):
        vecs[0, pl.ds(RHS * site, RHS), :] = rin[pl.ds(site, RHS, stride=SITES), :]

    def halves(i):
        for y in range(2):
            value = vecs[i, pl.ds(SLAB * y, SLAB), :]
            high, low = split(value)
            sent[i, y, 0], sent[i, y, 1] = high, low
            for at, shift in ((0, SLAB - RHS), (1, RHS)):
                moved = pltpu.roll(value, shift, 0)
                high, low = split(moved)
                local[at, y, 0], local[at, y, 1] = high, low

    def halo(i):
        plans = [
            (sent.at[i], big.at[i, 0], z_down),
            (sent.at[i], big.at[i, 1], z_up),
            (sent.at[i], big.at[i, 2], t_down),
            (sent.at[i], big.at[i, 3], t_up),
            (sent.at[i, 0], rows.at[i, 1], y_down),
            (sent.at[i, 1], rows.at[i, 0], y_up),
        ]
        return [
            pltpu.make_async_remote_copy(
                src_ref=src, dst_ref=dst, send_sem=send_sem.at[i, k], recv_sem=recv_sem.at[i, k],
                device_id=device, device_id_type=MESH,
            )
            for k, (src, dst, device) in enumerate(plans)
        ]

    def gram(i):
        lane = lax.broadcasted_iota(jnp.int32, (24, 128), 1)
        sign = jnp.where(lane < HALF, 1.0, -1.0)

        def one(j, total):
            left = vecs[i].reshape(8, 24, 128)
            right = vecs[j].reshape(8, 24, 128)
            turned = pltpu.roll(vecs[j], HALF, 1).reshape(8, 24, 128)
            real = jnp.sum(jnp.sum(left * right, 0), 1, keepdims=True)
            imag = jnp.sum(jnp.sum(left * turned, 0) * sign, 1, keepdims=True)
            entry = i * (i + 1) // 2 + j
            return total + jnp.where(lane == entry, real, 0.0) + jnp.where(lane == entry + 16, imag, 0.0)

        grams[...] = lax.fori_loop(0, i + 1, one, grams[...])

    def weights(y, h, directions):
        first = 8 * y + 4 * h
        return jnp.concatenate([hop[pl.ds(first, 4), d].reshape(256, 128) for d in directions], 1)

    def fields(views, h):
        at = pl.ds(PACK * h, PACK)
        return jnp.concatenate([paired(jnp.concatenate([v[0, at, :], v[1, at, :]], 0)) for v in views], 1)

    groups = [(y, h) for y in range(2) for h in range(2)]

    def early(i):
        for g, (y, h) in enumerate(groups):
            views = [sent.at[i, y], local.at[0, y], local.at[1, y], sent.at[i, 1 - y]]
            acc[g] = dot(fields(views, h), weights(y, h, [0, 1, 2, 3 + y]))

    def late(i):
        for g, (y, h) in enumerate(groups):
            views = [rows.at[i, y]] + [big.at[i, k, y] for k in range(4)]
            total = acc[g] + dot(fields(views, h), weights(y, h, [4 - y, 5, 6, 7, 8]))
            first = total[0:48] + total[48:96]
            second = total[96:144] + total[144:192]
            vecs[i + 1, pl.ds(SLAB * y + PACK * h, PACK), :] = unpack(first, second) * SCALE

    grams[...] = jnp.zeros((24, 128), F32)
    pl.semaphore_wait(barrier, len(greeted))

    def iteration(i, carry):
        halves(i)
        copies = halo(i)
        for copy in copies:
            copy.start()

        @pl.when(i == 0)
        def _():
            load_hop.wait()

        early(i)
        gram(i)
        for copy in copies:
            copy.wait_recv()
        late(i)
        for copy in copies:
            copy.wait_send()
        return carry

    lax.fori_loop(0, ITERS, iteration, 0)
    gram(ITERS)

    both = grams[...] + pltpu.roll(grams[...], RHS, 0)
    packed = both[0:8] + pltpu.roll(both[8:16], 32, 1) + pltpu.roll(both[16:24], 64, 1)
    message[0] = packed[0:4]

    def reduce_over(phase, partners, slots):
        copies = [
            pltpu.make_async_remote_copy(
                src_ref=message.at[phase], dst_ref=slots.at[k],
                send_sem=red_send.at[phase], recv_sem=red_recv.at[phase],
                device_id=device, device_id_type=MESH,
            )
            for k, device in enumerate(partners)
        ]
        for copy in copies:
            copy.start()
        return lambda: (
            pltpu.make_async_copy(slots, slots, red_recv.at[phase]).wait(),
            pltpu.make_async_copy(slots, slots, red_send.at[phase]).wait(),
        )

    finish = reduce_over(0, phase0, slots0)
    load_rest.wait()
    for site in range(SITES):
        rest_hi[site], rest_lo[site] = split(rest[site])
    finish()
    message[1] = message[0] + jnp.sum(slots0[...], 0)
    reduce_over(1, phase1, slots1)()
    message[2] = message[1] + jnp.sum(slots1[...], 0)
    reduce_over(2, phase2, slots2)()
    total = message[2] + jnp.sum(slots2[...], 0)
    wide_msg[0:4, :] = total
    wide_msg[4:8, :] = total
    table = wide_msg[...]

    def entry(e):
        return pltpu.roll(table, (128 - e) % 128, 1)

    g = {}
    for i in range(5):
        for j in range(i + 1):
            e = i * (i + 1) // 2 + j
            g[i, j] = (entry(e), entry(16 + e) if i != j else jnp.zeros((8, 128), F32))

    def times(a, b):
        return a[0] * b[0] - a[1] * b[1], a[0] * b[1] + a[1] * b[0]

    def minus(a, b):
        return a[0] - b[0], a[1] - b[1]

    alphas = []
    for k in range(ITERS):
        inner, power = g[1, 0], g[1, 1][0]
        alpha = (inner[0] / power, inner[1] / power)
        alphas.append(alpha)
        size = alpha[0] * alpha[0] + alpha[1] * alpha[1]
        if k == ITERS - 1:
            break
        top = 4 - k
        later = {}
        for i in range(1, top):
            for j in range(i + 1):
                ahead = g[i, j + 1] if j + 1 <= i else (g[j + 1, i][0], -g[j + 1, i][1])
                value = minus(g[i, j], times(alpha, ahead))
                value = minus(value, times((alpha[0], -alpha[1]), g[i + 1, j]))
                far = g[i + 1, j + 1]
                later[i, j] = (value[0] + size * far[0], value[1] + size * far[1])
        g = later

    one = (jnp.ones((8, 128), F32), jnp.zeros((8, 128), F32))
    residual = [one]
    iterate = []
    for alpha in alphas:
        scaled = (alpha[0] * SCALE, alpha[1] * SCALE)
        added = [times(scaled, c) for c in residual]
        iterate = [
            (a[0] + b[0], a[1] + b[1]) if b is not None else a
            for a, b in zip(added, iterate + [None] * (len(added) - len(iterate)))
        ]
        moved = [times(alpha, c) for c in residual]
        grown = [residual[0]]
        for j in range(1, len(residual)):
            grown.append(minus(residual[j], moved[j - 1]))
        grown.append((-moved[-1][0], -moved[-1][1]))
        residual = grown

    sub = lax.broadcasted_iota(jnp.int32, (8, 128), 0) < 4
    left_half = lax.broadcasted_iota(jnp.int32, (24, 128), 1) < HALF

    def spread(value):
        c0, c1, c2 = (jnp.broadcast_to(value[:, at : at + 1], (8, 128)) for at in (0, 32, 64))
        return jnp.concatenate([jnp.where(sub, c0, c2), jnp.where(sub, c1, c0), jnp.where(sub, c2, c1)], 0)

    def coefficient(pair):
        imag = spread(pair[1])
        return spread(pair[0])[None], jnp.where(left_half, -imag, imag)[None]

    def vector(j):
        return vecs[j].reshape(8, 24, 128), pltpu.roll(vecs[j], HALF, 1).reshape(8, 24, 128)

    last = vecs[0].reshape(8, 24, 128)
    field = jnp.zeros((8, 24, 128), F32)
    for j in range(5):
        plain, turned = vector(j)
        if j > 0:
            re, im = coefficient(residual[j])
            last = last + re * plain + im * turned
        if j < ITERS:
            re, im = coefficient(iterate[j])
            field = field + re * plain + im * turned
    last = last.reshape(ROWS, 128)
    field = field.reshape(ROWS, 128)

    for h in range(2):
        pieces = [split(last[SLAB * y + PACK * h : SLAB * y + PACK * (h + 1)]) for y in range(2)]
        both_rows = jnp.concatenate([paired(jnp.concatenate(p, 0)) for p in pieces], 1)
        high_rows = jnp.concatenate([paired(p[0]) for p in pieces], 1)

        def blocks(ref):
            return jnp.concatenate([ref[8 * y + 4 * h : 8 * y + 4 * h + 4].reshape(256, 128) for y in range(2)], 1)

        main = dot(both_rows, blocks(rest_hi))
        rest_part = dot(high_rows, blocks(rest_lo))
        first = main[0:48] + main[48:96] + rest_part[0:48]
        second = main[96:144] + main[144:192] + rest_part[48:96]
        value = unpack(first, second)
        value = value + pltpu.roll(value, PACK - RHS, 0)
        mine[:, 2 * h, :] = value[0:12]
        mine[:, 2 * h + 1, :] = value[24:36]

    other = (w, phi * 2 + (1 - pc))

    def gather(k, src, slot, device):
        return pltpu.make_async_remote_copy(
            src_ref=src, dst_ref=coarse_ref.at[slot], send_sem=gat_send.at[k], recv_sem=gat_recv.at[k],
            device_id=device, device_id_type=MESH,
        )

    first_hop = [gather(k, mine, n, (w, ((phi + k) % 4) * 2 + pc)) for k in (2, 1, 3)]
    first_hop.append(gather(0, mine, n, other))
    for copy in first_hop:
        copy.start()
    keep = pltpu.make_async_copy(mine, coarse_ref.at[n], out_sem.at[0])
    keep.start()
    for site in range(SITES):
        xout[pl.ds(site, RHS, stride=SITES), :] = field[RHS * site : RHS * (site + 1)]
    put_x = pltpu.make_async_copy(xout, x_ref, out_sem.at[1])
    put_x.start()
    second_hop = []
    for k, copy in zip((2, 1, 3), first_hop):
        copy.wait_recv()
        slot = ((phi + 4 - k) % 4) * 2 + pc
        second_hop.append(gather(4 + k, coarse_ref.at[slot], slot, other))
        second_hop[-1].start()
    first_hop[3].wait_recv()
    for copy in second_hop:
        copy.wait_recv()
    for copy in first_hop + second_hop:
        copy.wait_send()
    keep.wait()
    put_x.wait()


def per_device(right_side, hop_blocks, restriction):
    right = jnp.transpose(right_side[0], (1, 0, 2)).reshape(ROWS, 128)
    x, coarse = pl.pallas_call(
        body,
        out_shape=(jax.ShapeDtypeStruct((ROWS, 128), F32), jax.ShapeDtypeStruct((8, RHS, 4, 128), F32)),
        in_specs=[pl.BlockSpec(memory_space=pl.ANY)] * 3,
        out_specs=(pl.BlockSpec(memory_space=pl.ANY), pl.BlockSpec(memory_space=pltpu.VMEM)),
        scratch_shapes=[
            pltpu.VMEM((ROWS, 128), F32),
            pltpu.VMEM((SITES, 9, 64, 128), BF16),
            pltpu.VMEM((SITES, 64, 128), F32),
            pltpu.VMEM((ITERS + 1, ROWS, 128), F32),
            pltpu.VMEM((ITERS, 2, 2, SLAB, 128), BF16),
            pltpu.VMEM((2, 2, 2, SLAB, 128), BF16),
            pltpu.VMEM((ITERS, 4, 2, 2, SLAB, 128), BF16),
            pltpu.VMEM((ITERS, 2, 2, SLAB, 128), BF16),
            pltpu.VMEM((4, 192, 256), F32),
            pltpu.VMEM((24, 128), F32),
            pltpu.VMEM((3, 4, 128), F32),
            pltpu.VMEM((15, 4, 128), F32),
            pltpu.VMEM((7, 4, 128), F32),
            pltpu.VMEM((7, 4, 128), F32),
            pltpu.VMEM((8, 128), F32),
            pltpu.VMEM((SITES, 64, 128), BF16),
            pltpu.VMEM((SITES, 64, 128), BF16),
            pltpu.VMEM((RHS, 4, 128), F32),
            pltpu.VMEM((ROWS, 128), F32),
            pltpu.SemaphoreType.DMA((3,)),
            pltpu.SemaphoreType.DMA((ITERS, 6)),
            pltpu.SemaphoreType.DMA((ITERS, 6)),
            pltpu.SemaphoreType.DMA((3,)),
            pltpu.SemaphoreType.DMA((3,)),
            pltpu.SemaphoreType.DMA((8,)),
            pltpu.SemaphoreType.DMA((8,)),
            pltpu.SemaphoreType.DMA((2,)),
        ],
        compiler_params=pltpu.CompilerParams(
            collective_id=0, has_side_effects=True, vmem_limit_bytes=56 * 1024 * 1024
        ),
        cost_estimate=pl.CostEstimate(flops=500_000_000, bytes_accessed=4_000_000, transcendentals=0),
        name="smooth",
    )(right, hop_blocks[0], restriction[0])
    x = jnp.transpose(x.reshape(RHS, SITES, 128), (1, 0, 2))[None]
    return x, jnp.transpose(coarse, (0, 2, 1, 3))


def solution(mesh):
    placed = (
        P("narrow", "wide", None, None),
        P("narrow", "wide", None, None, None),
        P("narrow", "wide", None, None),
    )
    return jax.shard_map(
        per_device,
        mesh=mesh,
        in_specs=placed,
        out_specs=(P("narrow", "wide", None, None), P(None, "wide", None, None)),
        check_vma=False,
    )
```

```python
import jax
import jax.numpy as jnp
from jax import lax
from jax.experimental import pallas as pl
from jax.experimental.pallas import tpu as pltpu
from jax.sharding import PartitionSpec as P

F32, BF16 = jnp.float32, jnp.bfloat16
MESH = pl.DeviceIdType.MESH
ITERS = 4
RHS = 12
SITES = 16
HALF = 64
ROWS = SITES * RHS
SLAB = ROWS // 2
PACK = 4 * RHS
SCALE = 1.0 / 16.0


def dot(lhs, rhs):
    return lax.dot_general(lhs, rhs, (((1,), (1,)), ((), ())), preferred_element_type=F32)


def split(value):
    high = value.astype(BF16)
    return high, (value - high.astype(F32)).astype(BF16)


def paired(rows):
    lane = lax.broadcasted_iota(jnp.int32, rows.shape, 1)
    sign = jnp.where(lane < HALF, 1.0, -1.0).astype(rows.dtype)
    return jnp.concatenate([rows * sign, pltpu.roll(rows, HALF, 1)], 0)


def unpack(first, second):
    first = jnp.concatenate([first[0:24, 0:128], first[24:48, 128:256]], 0)
    second = jnp.concatenate([second[0:24, 0:128], second[24:48, 128:256]], 0)
    row = lax.broadcasted_iota(jnp.int32, (PACK, 128), 0)
    lane = lax.broadcasted_iota(jnp.int32, (PACK, 128), 1)
    even = (row < 12) | ((row >= 24) & (row < 36))
    moved = pltpu.roll(jnp.where(even, second, first), HALF, 1)
    return jnp.where(even == (lane < HALF), jnp.where(even, first, second), moved)


def body(
    right_ref, hop_ref, rest_ref, x_ref, coarse_ref,
    rin, hop, rest, vecs, sent, local, big, rows, acc, grams, message, slots0, slots1, slots2, wide_msg,
    rest_hi, rest_lo, mine, posted, xout,
    load_sem, send_sem, recv_sem, red_send, red_recv, gat_send, gat_recv, out_sem,
):
    w = lax.axis_index("wide")
    n = lax.axis_index("narrow")
    ylat, zlat = w % 8, w // 8
    px, pz, plo = w % 8, (w // 8) % 8, w // 64
    phi, pc = n // 2, n % 2
    py = phi * 2 + plo

    load_right = pltpu.make_async_copy(right_ref, rin, load_sem.at[0])
    load_right.start()
    load_hop = pltpu.make_async_copy(hop_ref, hop, load_sem.at[1])
    load_hop.start()
    load_rest = pltpu.make_async_copy(rest_ref, rest, load_sem.at[2])
    load_rest.start()

    z_up, z_down = (((zlat + 1) % 16) * 8 + ylat, n), (((zlat + 15) % 16) * 8 + ylat, n)
    y_up, y_down = (zlat * 8 + (ylat + 1) % 8, n), (zlat * 8 + (ylat + 7) % 8, n)
    t_up, t_down = (w, (n + 1) % 8), (w, (n + 7) % 8)

    other = (w, phi * 2 + (1 - pc))

    def at_xy(offset):
        return ((w // 8) * 8 + (px + offset) % 8, ((phi + offset // 8) % 4) * 2 + pc)

    def at_zy(offset):
        return (((plo + offset // 8) % 2) * 64 + ((pz + offset) % 8) * 8 + px, n)

    wide_steps = [1 + k + 15 * pc for k in range(16)]
    deep_steps = [1 + k + 7 * pc for k in range(8)]

    def back_xy(offset):
        return ((w // 8) * 8 + (px + 64 - offset) % 8, ((phi + 4 - offset // 8) % 4) * 2 + pc)

    def back_zy(offset):
        return (((plo + 2 - offset // 8) % 2) * 64 + ((pz + 64 - offset) % 8) * 8 + px, n)

    gathered = [(w, ((phi + k) % 4) * 2 + pc) for k in (2, 1, 3)]
    greeted = [z_up, z_down, t_up, t_down, y_up, y_down, other] + gathered
    greeted += [back_xy(o) for o in wide_steps] + [back_zy(o) for o in deep_steps]
    barrier = pltpu.get_barrier_semaphore()
    for device in greeted:
        pl.semaphore_signal(barrier, inc=1, device_id=device, device_id_type=MESH)

    load_right.wait()
    for site in range(SITES):
        vecs[0, pl.ds(RHS * site, RHS), :] = rin[pl.ds(site, RHS, stride=SITES), :]

    def outgoing(i):
        for y in range(2):
            sent[i, y, 0], sent[i, y, 1] = split(vecs[i, pl.ds(SLAB * y, SLAB), :])

    def shifted(i):
        for y in range(2):
            value = vecs[i, pl.ds(SLAB * y, SLAB), :]
            for at, shift in ((0, SLAB - RHS), (1, RHS)):
                local[at, y, 0], local[at, y, 1] = split(pltpu.roll(value, shift, 0))

    def halo(i):
        plans = [
            (sent.at[i], big.at[i, 0], z_down),
            (sent.at[i], big.at[i, 1], z_up),
            (sent.at[i], big.at[i, 2], t_down),
            (sent.at[i], big.at[i, 3], t_up),
            (sent.at[i, 0], rows.at[i, 1], y_down),
            (sent.at[i, 1], rows.at[i, 0], y_up),
        ]
        return [
            pltpu.make_async_remote_copy(
                src_ref=src, dst_ref=dst, send_sem=send_sem.at[i, k], recv_sem=recv_sem.at[i, k],
                device_id=device, device_id_type=MESH,
            )
            for k, (src, dst, device) in enumerate(plans)
        ]

    def gram(i):
        lane = lax.broadcasted_iota(jnp.int32, (24, 128), 1)
        sign = jnp.where(lane < HALF, -1.0, 1.0)[None]
        left = vecs[i].reshape(8, 24, 128)
        turned = pltpu.roll(vecs[i], HALF, 1).reshape(8, 24, 128) * sign

        def one(j, total):
            right = vecs[j].reshape(8, 24, 128)
            real = jnp.sum(jnp.sum(left * right, 0), 1, keepdims=True)
            imag = jnp.sum(jnp.sum(turned * right, 0), 1, keepdims=True)
            entry = i * (i + 1) // 2 + j
            return total + jnp.where(lane == entry, real, 0.0) + jnp.where(lane == entry + 16, imag, 0.0)

        if isinstance(i, int):
            total = grams[...]
            for j in range(i + 1):
                total = one(j, total)
            return total
        grams[...] = lax.fori_loop(0, i + 1, one, grams[...])

    def weights(y, h, directions):
        first = 8 * y + 4 * h
        return jnp.concatenate([hop[pl.ds(first, 4), d].reshape(256, 128) for d in directions], 1)

    def fields(views, h):
        at = pl.ds(PACK * h, PACK)
        return jnp.concatenate([paired(jnp.concatenate([v[0, at, :], v[1, at, :]], 0)) for v in views], 1)

    groups = [(y, h) for y in range(2) for h in range(2)]

    def early(i):
        for g, (y, h) in enumerate(groups):
            views = [sent.at[i, y], local.at[0, y], local.at[1, y], sent.at[i, 1 - y]]
            acc[g] = dot(fields(views, h), weights(y, h, [0, 1, 2, 3 + y]))

    def middle(i):
        for g, (y, h) in enumerate(groups):
            views = [rows.at[i, y], big.at[i, 0, y], big.at[i, 1, y]]
            acc[g] += dot(fields(views, h), weights(y, h, [4 - y, 5, 6]))

    def late(i):
        for g, (y, h) in enumerate(groups):
            views = [big.at[i, 2, y], big.at[i, 3, y]]
            total = acc[g] + dot(fields(views, h), weights(y, h, [7, 8]))
            first = total[0:48] + total[48:96]
            second = total[96:144] + total[144:192]
            vecs[i + 1, pl.ds(SLAB * y + PACK * h, PACK), :] = unpack(first, second) * SCALE

    grams[...] = jnp.zeros((24, 128), F32)
    outgoing(0)
    pl.semaphore_wait(barrier, len(greeted))

    def iteration(i, carry):
        copies = halo(i)
        for copy in copies:
            copy.start()
        shifted(i)

        @pl.when(i == 0)
        def _():
            load_hop.wait()

        early(i)
        gram(i)
        for k in (4, 5, 0, 1):
            copies[k].wait_recv()
        middle(i)
        for k in (2, 3):
            copies[k].wait_recv()
        late(i)

        @pl.when(i < ITERS - 1)
        def _():
            outgoing(i + 1)

        return carry

    lax.fori_loop(0, ITERS, iteration, 0)
    sums = gram(ITERS)

    both = sums + pltpu.roll(sums, RHS, 0)
    packed = both[0:8] + pltpu.roll(both[8:16], 32, 1) + pltpu.roll(both[16:24], 64, 1)
    message[0] = packed[0:4]

    def reduce_over(phase, partners, slots):
        copies = [
            pltpu.make_async_remote_copy(
                src_ref=message.at[phase], dst_ref=slots.at[k],
                send_sem=red_send.at[phase], recv_sem=red_recv.at[phase],
                device_id=device, device_id_type=MESH,
            )
            for k, device in enumerate(partners)
        ]
        for copy in copies:
            copy.start()
        return [pltpu.make_async_copy(slots, slots, sem.at[phase]) for sem in (red_recv, red_send)]

    def part(own, slots):
        return jnp.sum(slots[1:], 0) + jnp.where(pc == 0, own + slots[0], 0.0)

    waits = [reduce_over(0, [other], slots0.at[0:1])]
    load_rest.wait()
    waits[0][0].wait()
    message[1] = message[0] + slots0[0]
    waits.append(reduce_over(1, [at_xy(o) for o in wide_steps], slots1))
    for site in range(SITES):
        rest_hi[site], rest_lo[site] = split(rest[site])
    waits[1][0].wait()
    message[2] = part(message[1], slots1[...])
    waits.append(reduce_over(2, [other], slots0.at[1:2]))
    waits[2][0].wait()
    message[3] = message[2] + slots0[1]
    waits.append(reduce_over(3, [at_zy(o) for o in deep_steps], slots2))

    def drain(i, carry):
        for copy in halo(i):
            copy.wait_send()
        return carry

    lax.fori_loop(0, ITERS, drain, 0)
    waits[3][0].wait()
    message[4] = part(message[3], slots2[...])
    waits.append(reduce_over(4, [other], slots0.at[2:3]))
    for wait in waits[:4]:
        wait[1].wait()
    waits[4][0].wait()
    total = message[4] + slots0[2]
    wide_msg[0:4, :] = total
    wide_msg[4:8, :] = total
    table = wide_msg[...]

    def entry(e):
        return pltpu.roll(table, (128 - e) % 128, 1)

    g = {}
    for i in range(5):
        for j in range(i + 1):
            e = i * (i + 1) // 2 + j
            g[i, j] = (entry(e), entry(16 + e) if i != j else jnp.zeros((8, 128), F32))

    def times(a, b):
        return a[0] * b[0] - a[1] * b[1], a[0] * b[1] + a[1] * b[0]

    def minus(a, b):
        return a[0] - b[0], a[1] - b[1]

    alphas = []
    for k in range(ITERS):
        inner, power = g[1, 0], g[1, 1][0]
        alpha = (inner[0] / power, inner[1] / power)
        alphas.append(alpha)
        size = alpha[0] * alpha[0] + alpha[1] * alpha[1]
        if k == ITERS - 1:
            break
        top = 4 - k
        later = {}
        for i in range(1, top):
            for j in range(i + 1):
                ahead = g[i, j + 1] if j + 1 <= i else (g[j + 1, i][0], -g[j + 1, i][1])
                value = minus(g[i, j], times(alpha, ahead))
                value = minus(value, times((alpha[0], -alpha[1]), g[i + 1, j]))
                far = g[i + 1, j + 1]
                later[i, j] = (value[0] + size * far[0], value[1] + size * far[1])
        g = later

    one = (jnp.ones((8, 128), F32), jnp.zeros((8, 128), F32))
    residual = [one]
    iterate = []
    for alpha in alphas:
        scaled = (alpha[0] * SCALE, alpha[1] * SCALE)
        added = [times(scaled, c) for c in residual]
        iterate = [
            (a[0] + b[0], a[1] + b[1]) if b is not None else a
            for a, b in zip(added, iterate + [None] * (len(added) - len(iterate)))
        ]
        moved = [times(alpha, c) for c in residual]
        grown = [residual[0]]
        for j in range(1, len(residual)):
            grown.append(minus(residual[j], moved[j - 1]))
        grown.append((-moved[-1][0], -moved[-1][1]))
        residual = grown

    sub = lax.broadcasted_iota(jnp.int32, (8, 128), 0) < 4
    left_half = lax.broadcasted_iota(jnp.int32, (24, 128), 1) < HALF

    def spread(value):
        c0, c1, c2 = (jnp.broadcast_to(value[:, at : at + 1], (8, 128)) for at in (0, 32, 64))
        return jnp.concatenate([jnp.where(sub, c0, c2), jnp.where(sub, c1, c0), jnp.where(sub, c2, c1)], 0)

    def coefficient(pair):
        imag = spread(pair[1])
        return spread(pair[0])[None], jnp.where(left_half, -imag, imag)[None]

    def vector(j):
        return vecs[j].reshape(8, 24, 128), pltpu.roll(vecs[j], HALF, 1).reshape(8, 24, 128)

    last = vecs[0].reshape(8, 24, 128)
    field = jnp.zeros((8, 24, 128), F32)
    for j in range(5):
        plain, turned = vector(j)
        if j > 0:
            re, im = coefficient(residual[j])
            last = last + re * plain + im * turned
        if j < ITERS:
            re, im = coefficient(iterate[j])
            field = field + re * plain + im * turned
    last = last.reshape(ROWS, 128)
    field = field.reshape(ROWS, 128)

    for h in range(2):
        pieces = [split(last[SLAB * y + PACK * h : SLAB * y + PACK * (h + 1)]) for y in range(2)]
        both_rows = jnp.concatenate([paired(jnp.concatenate(p, 0)) for p in pieces], 1)
        high_rows = jnp.concatenate([paired(p[0]) for p in pieces], 1)

        def blocks(ref):
            return jnp.concatenate([ref[8 * y + 4 * h : 8 * y + 4 * h + 4].reshape(256, 128) for y in range(2)], 1)

        main = dot(both_rows, blocks(rest_hi))
        rest_part = dot(high_rows, blocks(rest_lo))
        first = main[0:48] + main[48:96] + rest_part[0:48]
        second = main[96:144] + main[144:192] + rest_part[48:96]
        value = unpack(first, second)
        value = value + pltpu.roll(value, PACK - RHS, 0)
        mine[pl.ds(2 * h, RHS, stride=4), :] = value[0:12]
        mine[pl.ds(2 * h + 1, RHS, stride=4), :] = value[24:36]
    posted[n] = mine[...].astype(BF16)

    def gather(k, slot, device):
        return pltpu.make_async_remote_copy(
            src_ref=posted.at[slot], dst_ref=posted.at[slot], send_sem=gat_send.at[k], recv_sem=gat_recv.at[k],
            device_id=device, device_id_type=MESH,
        )

    first_hop = [gather(k, n, device) for k, device in zip((2, 1, 3), gathered)]
    first_hop.append(gather(0, n, other))
    for copy in first_hop:
        copy.start()
    for site in range(SITES):
        xout[pl.ds(site, RHS, stride=SITES), :] = field[RHS * site : RHS * (site + 1)]
    put_x = pltpu.make_async_copy(xout, x_ref, out_sem.at[0])
    put_x.start()
    second_hop = []
    for k, copy in zip((1, 3, 2), (first_hop[1], first_hop[2], first_hop[0])):
        copy.wait_recv()
        second_hop.append(gather(4 + k, ((phi + 4 - k) % 4) * 2 + pc, other))
        second_hop[-1].start()
    first_hop[3].wait_recv()
    for copy in second_hop:
        copy.wait_recv()
    coarse_ref[...] = posted[...].astype(F32)
    for copy in first_hop + second_hop:
        copy.wait_send()
    waits[4][1].wait()
    put_x.wait()


def hand_over(x_in, coarse_in, x_out, coarse_out):
    x_out[...] = x_in[...]
    coarse_out[...] = coarse_in[...]


def per_device(right_side, hop_blocks, restriction):
    right = jnp.transpose(right_side[0], (1, 0, 2)).reshape(ROWS, 128)
    shapes = (jax.ShapeDtypeStruct((ROWS, 128), F32), jax.ShapeDtypeStruct((8, 4 * RHS, 128), F32))
    held = pl.pallas_call(
        body,
        out_shape=shapes,
        in_specs=[pl.BlockSpec(memory_space=pl.ANY)] * 3,
        out_specs=(pl.BlockSpec(memory_space=pl.ANY), pl.BlockSpec(memory_space=pltpu.VMEM)),
        scratch_shapes=[
            pltpu.VMEM((ROWS, 128), F32),
            pltpu.VMEM((SITES, 9, 64, 128), BF16),
            pltpu.VMEM((SITES, 64, 128), F32),
            pltpu.VMEM((ITERS + 1, ROWS, 128), F32),
            pltpu.VMEM((ITERS, 2, 2, SLAB, 128), BF16),
            pltpu.VMEM((2, 2, 2, SLAB, 128), BF16),
            pltpu.VMEM((ITERS, 4, 2, 2, SLAB, 128), BF16),
            pltpu.VMEM((ITERS, 2, 2, SLAB, 128), BF16),
            pltpu.VMEM((4, 192, 256), F32),
            pltpu.VMEM((24, 128), F32),
            pltpu.VMEM((5, 4, 128), F32),
            pltpu.VMEM((3, 4, 128), F32),
            pltpu.VMEM((16, 4, 128), F32),
            pltpu.VMEM((8, 4, 128), F32),
            pltpu.VMEM((8, 128), F32),
            pltpu.VMEM((SITES, 64, 128), BF16),
            pltpu.VMEM((SITES, 64, 128), BF16),
            pltpu.VMEM((4 * RHS, 128), F32),
            pltpu.VMEM((8, 4 * RHS, 128), BF16),
            pltpu.VMEM((ROWS, 128), F32),
            pltpu.SemaphoreType.DMA((3,)),
            pltpu.SemaphoreType.DMA((ITERS, 6)),
            pltpu.SemaphoreType.DMA((ITERS, 6)),
            pltpu.SemaphoreType.DMA((5,)),
            pltpu.SemaphoreType.DMA((5,)),
            pltpu.SemaphoreType.DMA((8,)),
            pltpu.SemaphoreType.DMA((8,)),
            pltpu.SemaphoreType.DMA((1,)),
        ],
        compiler_params=pltpu.CompilerParams(
            collective_id=0, has_side_effects=True, vmem_limit_bytes=56 * 1024 * 1024
        ),
        cost_estimate=pl.CostEstimate(flops=500_000_000, bytes_accessed=4_000_000, transcendentals=0),
        name="smooth",
    )(right, hop_blocks[0], restriction[0])
    x, coarse = pl.pallas_call(
        hand_over,
        out_shape=shapes,
        in_specs=[pl.BlockSpec(memory_space=pltpu.VMEM)] * 2,
        out_specs=(pl.BlockSpec(memory_space=pltpu.VMEM),) * 2,
        name="hand_over",
    )(*held)
    x = jnp.transpose(x.reshape(RHS, SITES, 128), (1, 0, 2))[None]
    return x, jnp.transpose(coarse.reshape(8, RHS, 4, 128), (0, 2, 1, 3))


def solution(mesh):
    placed = (
        P("narrow", "wide", None, None),
        P("narrow", "wide", None, None, None),
        P("narrow", "wide", None, None),
    )
    return jax.shard_map(
        per_device,
        mesh=mesh,
        in_specs=placed,
        out_specs=(P("narrow", "wide", None, None), P(None, "wide", None, None)),
        check_vma=False,
    )
```

```python
import jax
import jax.numpy as jnp
from jax import lax
from jax.experimental import pallas as pl
from jax.experimental.pallas import tpu as pltpu
from jax.sharding import PartitionSpec as P

F32, BF16 = jnp.float32, jnp.bfloat16
MESH = pl.DeviceIdType.MESH
ITERS = 4
RHS = 12
SITES = 16
HALF = 64
ROWS = SITES * RHS
SLAB = ROWS // 2
PACK = 4 * RHS
SCALE = 1.0 / 16.0


def dot(lhs, rhs):
    return lax.dot_general(lhs, rhs, (((1,), (1,)), ((), ())), preferred_element_type=F32)


def mod(value, size):
    return lax.rem(value, jnp.int32(size))


def div(value, size):
    return lax.div(value, jnp.int32(size))


def split(value):
    high = value.astype(BF16)
    return high, (value - high.astype(F32)).astype(BF16)


def paired(rows):
    lane = lax.broadcasted_iota(jnp.int32, rows.shape, 1)
    sign = jnp.where(lane < HALF, 1.0, -1.0).astype(rows.dtype)
    return jnp.concatenate([rows * sign, pltpu.roll(rows, HALF, 1)], 0)


def unpack(first, second):
    first = jnp.concatenate([first[0:24, 0:128], first[24:48, 128:256]], 0)
    second = jnp.concatenate([second[0:24, 0:128], second[24:48, 128:256]], 0)
    row = lax.broadcasted_iota(jnp.int32, (PACK, 128), 0)
    lane = lax.broadcasted_iota(jnp.int32, (PACK, 128), 1)
    even = (row < 12) | ((row >= 24) & (row < 36))
    moved = pltpu.roll(jnp.where(even, second, first), HALF, 1)
    return jnp.where(even == (lane < HALF), jnp.where(even, first, second), moved)


def body(
    right_ref, hop_ref, rest_ref, x_ref, coarse_ref,
    rin, hop, rest, vecs, sent, local, big, rows, acc, grams, message, slots0, slots1, slots2, wide_msg,
    coarse, rest_hi, rest_lo, mine, posted, xout,
    load_sem, send_sem, recv_sem, red_send, red_recv, gat_send, gat_recv, out_sem,
):
    w = lax.axis_index("wide")
    n = lax.axis_index("narrow")
    px, zlat = mod(w, 8), div(w, 8)
    pz, plo = mod(zlat, 8), div(w, 64)
    phi, pc = div(n, 2), mod(n, 2)

    load_right = pltpu.make_async_copy(right_ref, rin, load_sem.at[0])
    load_right.start()
    load_hop = pltpu.make_async_copy(hop_ref, hop, load_sem.at[1])
    load_hop.start()
    load_rest = pltpu.make_async_copy(rest_ref, rest, load_sem.at[2])
    load_rest.start()

    in_x = [zlat * 8 + mod(px + d, 8) for d in range(8)]
    in_z = [mod(pz + d, 8) * 8 + px for d in range(8)]
    in_time = [mod(phi + d, 4) * 2 + pc for d in range(4)]

    z_up, z_down = (mod(zlat + 1, 16) * 8 + px, n), (mod(zlat + 15, 16) * 8 + px, n)
    y_up, y_down = (in_x[1], n), (in_x[7], n)
    t_up, t_down = (w, mod(n + 1, 8)), (w, mod(n + 7, 8))
    other = (w, n + 1 - 2 * pc)

    ahead = [mod(phi + 2 * pc, 4) * 2 + pc, mod(phi + 2 * pc + 1, 4) * 2 + pc]
    behind = [mod(phi + 4 - 2 * pc, 4) * 2 + pc, mod(phi + 3 - 2 * pc, 4) * 2 + pc]
    wide_to = [(w, in_time[2])] + [(in_x[k % 8], ahead[k // 8]) for k in range(1, 16)]
    wide_from = [(w, in_time[2])] + [(in_x[(8 - k) % 8], behind[k // 8]) for k in range(1, 16)]
    half = mod(plo + pc, 2) * 64
    deep_to = [(in_z[0] + 64 - 64 * plo, n)] + [(in_z[k] + half, n) for k in range(1, 8)]
    deep_from = [deep_to[0]] + [(in_z[8 - k] + half, n) for k in range(1, 8)]

    gathered = [(w, in_time[k]) for k in (2, 1, 3)]
    greeted = [z_up, z_down, t_up, t_down, y_up, y_down, (w, mod(phi + 1 + 2 * pc, 4) * 2 + pc)]
    greeted += wide_from + deep_from
    barrier = pltpu.get_barrier_semaphore()
    for device in greeted:
        pl.semaphore_signal(barrier, inc=1, device_id=device, device_id_type=MESH)

    load_right.wait()
    for site in range(SITES):
        vecs[0, pl.ds(RHS * site, RHS), :] = rin[pl.ds(site, RHS, stride=SITES), :]

    def outgoing(i):
        for y in range(2):
            sent[i, y, 0], sent[i, y, 1] = split(vecs[i, pl.ds(SLAB * y, SLAB), :])

    def shifted(i):
        for y in range(2):
            value = vecs[i, pl.ds(SLAB * y, SLAB), :]
            for at, shift in ((0, SLAB - RHS), (1, RHS)):
                local[at, y, 0], local[at, y, 1] = split(pltpu.roll(value, shift, 0))

    def halo(i):
        plans = [
            (sent.at[i], big.at[i, 0], z_down),
            (sent.at[i], big.at[i, 1], z_up),
            (sent.at[i], big.at[i, 2], t_down),
            (sent.at[i], big.at[i, 3], t_up),
            (sent.at[i, 0], rows.at[i, 1], y_down),
            (sent.at[i, 1], rows.at[i, 0], y_up),
        ]
        return [
            pltpu.make_async_remote_copy(
                src_ref=src, dst_ref=dst, send_sem=send_sem.at[i, k], recv_sem=recv_sem.at[i, k],
                device_id=device, device_id_type=MESH,
            )
            for k, (src, dst, device) in enumerate(plans)
        ]

    def gram(i):
        lane = lax.broadcasted_iota(jnp.int32, (24, 128), 1)
        sign = jnp.where(lane < HALF, -1.0, 1.0)[None]
        left = vecs[i].reshape(8, 24, 128)
        turned = pltpu.roll(vecs[i], HALF, 1).reshape(8, 24, 128) * sign

        def one(j, total):
            right = vecs[j].reshape(8, 24, 128)
            real = jnp.sum(jnp.sum(left * right, 0), 1, keepdims=True)
            imag = jnp.sum(jnp.sum(turned * right, 0), 1, keepdims=True)
            entry = i * (i + 1) // 2 + j
            return total + jnp.where(lane == entry, real, 0.0) + jnp.where(lane == entry + 16, imag, 0.0)

        if isinstance(i, int):
            total = grams[...]
            for j in range(i + 1):
                total = one(j, total)
            return total
        grams[...] = lax.fori_loop(0, i + 1, one, grams[...])

    def weights(y, h, directions):
        first = 8 * y + 4 * h
        return jnp.concatenate([hop[pl.ds(first, 4), d].reshape(256, 128) for d in directions], 1)

    def fields(views, h):
        at = pl.ds(PACK * h, PACK)
        return jnp.concatenate([paired(jnp.concatenate([v[0, at, :], v[1, at, :]], 0)) for v in views], 1)

    groups = [(y, h) for y in range(2) for h in range(2)]

    def early(i):
        for g, (y, h) in enumerate(groups):
            views = [sent.at[i, y], local.at[0, y], local.at[1, y], sent.at[i, 1 - y]]
            acc[g] = dot(fields(views, h), weights(y, h, [0, 1, 2, 3 + y]))

    def middle(i):
        for g, (y, h) in enumerate(groups):
            views = [rows.at[i, y], big.at[i, 0, y], big.at[i, 1, y]]
            acc[g] += dot(fields(views, h), weights(y, h, [4 - y, 5, 6]))

    def late(i):
        for g, (y, h) in enumerate(groups):
            views = [big.at[i, 2, y], big.at[i, 3, y]]
            total = acc[g] + dot(fields(views, h), weights(y, h, [7, 8]))
            first = total[0:48] + total[48:96]
            second = total[96:144] + total[144:192]
            vecs[i + 1, pl.ds(SLAB * y + PACK * h, PACK), :] = unpack(first, second) * SCALE

    grams[...] = jnp.zeros((24, 128), F32)
    outgoing(0)
    pl.semaphore_wait(barrier, len(greeted))

    def iteration(i, carry):
        copies = halo(i)
        for copy in copies:
            copy.start()
        shifted(i)

        @pl.when(i == 0)
        def _():
            load_hop.wait()

        @pl.when(i == 1)
        def _():
            load_rest.wait()
            for site in range(SITES):
                rest_hi[site], rest_lo[site] = split(rest[site])

        early(i)
        gram(i)
        for k in (4, 5, 0, 1):
            copies[k].wait_recv()
        middle(i)
        for k in (2, 3):
            copies[k].wait_recv()
        late(i)

        @pl.when(i < ITERS - 1)
        def _():
            outgoing(i + 1)

        return carry

    lax.fori_loop(0, ITERS, iteration, 0)
    sums = gram(ITERS)

    both = sums + pltpu.roll(sums, RHS, 0)
    packed = both[0:8] + pltpu.roll(both[8:16], 32, 1) + pltpu.roll(both[16:24], 64, 1)
    message[0] = packed[0:4]

    def reduce_over(phase, partners, slots):
        copies = [
            pltpu.make_async_remote_copy(
                src_ref=message.at[phase], dst_ref=slots.at[k],
                send_sem=red_send.at[phase], recv_sem=red_recv.at[phase],
                device_id=device, device_id_type=MESH,
            )
            for k, device in enumerate(partners)
        ]
        for copy in copies:
            copy.start()
        return [pltpu.make_async_copy(slots, slots, sem.at[phase]) for sem in (red_recv, red_send)]

    def part(own, slots):
        return jnp.sum(slots[1:], 0) + jnp.where(pc == 0, own, slots[0])

    def restrict(j):
        pieces = []
        for h in range(2):
            rows_of = [split(vecs[j, pl.ds(SLAB * y + PACK * h, PACK), :]) for y in range(2)]
            both_rows = jnp.concatenate([paired(jnp.concatenate(p, 0)) for p in rows_of], 1)
            high_rows = jnp.concatenate([paired(p[0]) for p in rows_of], 1)

            def blocks(ref):
                return jnp.concatenate([ref[8 * y + 4 * h : 8 * y + 4 * h + 4].reshape(256, 128) for y in range(2)], 1)

            main = dot(both_rows, blocks(rest_hi))
            remainder = dot(high_rows, blocks(rest_lo))
            first = main[0:48] + main[48:96] + remainder[0:48]
            second = main[96:144] + main[144:192] + remainder[48:96]
            value = unpack(first, second)
            value = value + pltpu.roll(value, PACK - RHS, 0)
            pieces += [value[0:12], value[24:36]]
        coarse[j] = jnp.concatenate(pieces, 0)

    def restrict_some(start, stop):
        def one(j, carry):
            restrict(j)
            return carry

        lax.fori_loop(start, stop, one, 0)

    waits = [reduce_over(0, [other], slots0.at[0:1])]
    waits[0][0].wait()
    message[1] = message[0] + slots0[0]
    waits.append(reduce_over(1, wide_to, slots1))
    restrict_some(0, 3)
    waits[1][0].wait()
    message[2] = part(message[1], slots1[...])
    waits.append(reduce_over(2, [other], slots0.at[1:2]))
    waits[2][0].wait()
    message[3] = message[2] + slots0[1]
    waits.append(reduce_over(3, deep_to, slots2))

    def drain(i, carry):
        for copy in halo(i):
            copy.wait_send()
        return carry

    restrict_some(3, 5)
    waits[3][0].wait()
    message[4] = part(message[3], slots2[...])
    waits.append(reduce_over(4, [other], slots0.at[2:3]))
    waits[4][0].wait()
    total = message[4] + slots0[2]
    wide_msg[0:4, :] = total
    wide_msg[4:8, :] = total
    table = wide_msg[...]

    def entry(e):
        return pltpu.roll(table, (128 - e) % 128, 1)

    g = {}
    for i in range(5):
        for j in range(i + 1):
            e = i * (i + 1) // 2 + j
            g[i, j] = (entry(e), entry(16 + e) if i != j else jnp.zeros((8, 128), F32))

    def times(a, b):
        return a[0] * b[0] - a[1] * b[1], a[0] * b[1] + a[1] * b[0]

    def minus(a, b):
        return a[0] - b[0], a[1] - b[1]

    alphas = []
    for k in range(ITERS):
        inner, power = g[1, 0], g[1, 1][0]
        alpha = (inner[0] / power, inner[1] / power)
        alphas.append(alpha)
        size = alpha[0] * alpha[0] + alpha[1] * alpha[1]
        if k == ITERS - 1:
            break
        top = 4 - k
        later = {}
        for i in range(1, top):
            for j in range(i + 1):
                ahead = g[i, j + 1] if j + 1 <= i else (g[j + 1, i][0], -g[j + 1, i][1])
                value = minus(g[i, j], times(alpha, ahead))
                value = minus(value, times((alpha[0], -alpha[1]), g[i + 1, j]))
                far = g[i + 1, j + 1]
                later[i, j] = (value[0] + size * far[0], value[1] + size * far[1])
        g = later

    one = (jnp.ones((8, 128), F32), jnp.zeros((8, 128), F32))
    residual = [one]
    iterate = []
    for alpha in alphas:
        scaled = (alpha[0] * SCALE, alpha[1] * SCALE)
        added = [times(scaled, c) for c in residual]
        iterate = [
            (a[0] + b[0], a[1] + b[1]) if b is not None else a
            for a, b in zip(added, iterate + [None] * (len(added) - len(iterate)))
        ]
        moved = [times(alpha, c) for c in residual]
        grown = [residual[0]]
        for j in range(1, len(residual)):
            grown.append(minus(residual[j], moved[j - 1]))
        grown.append((-moved[-1][0], -moved[-1][1]))
        residual = grown

    sub = lax.broadcasted_iota(jnp.int32, (8, 128), 0) < 4
    left_half = lax.broadcasted_iota(jnp.int32, (24, 128), 1) < HALF

    def spread(value):
        c0, c1, c2 = (jnp.broadcast_to(value[:, at : at + 1], (8, 128)) for at in (0, 32, 64))
        return jnp.concatenate([jnp.where(sub, c0, c2), jnp.where(sub, c1, c0), jnp.where(sub, c2, c1)], 0)

    def coefficient(pair):
        imag = spread(pair[1])
        return spread(pair[0])[None], jnp.where(left_half, -imag, imag)[None]

    last = coarse[0].reshape(2, 24, 128)
    for j in range(1, 5):
        re, im = coefficient(residual[j])
        last = last + re * coarse[j].reshape(2, 24, 128)
        last = last + im * pltpu.roll(coarse[j], HALF, 1).reshape(2, 24, 128)
    last = last.reshape(PACK, 128)
    for at in range(4):
        mine[pl.ds(at, RHS, stride=4), :] = last[RHS * at : RHS * (at + 1)]
    posted[n] = mine[...].astype(BF16)

    def gather(k, slot, device):
        return pltpu.make_async_remote_copy(
            src_ref=posted.at[slot], dst_ref=posted.at[slot], send_sem=gat_send.at[k], recv_sem=gat_recv.at[k],
            device_id=device, device_id_type=MESH,
        )

    first_hop = [gather(k, n, device) for k, device in zip((2, 1, 3), gathered)]
    first_hop.append(gather(0, n, other))
    for copy in first_hop:
        copy.start()
    field = jnp.zeros((8, 24, 128), F32)
    for j in range(ITERS):
        re, im = coefficient(iterate[j])
        field = field + re * vecs[j].reshape(8, 24, 128)
        field = field + im * pltpu.roll(vecs[j], HALF, 1).reshape(8, 24, 128)
    field = field.reshape(ROWS, 128)
    for site in range(SITES):
        xout[pl.ds(site, RHS, stride=SITES), :] = field[RHS * site : RHS * (site + 1)]
    put_x = pltpu.make_async_copy(xout, x_ref, out_sem.at[0])
    put_x.start()
    lax.fori_loop(0, ITERS, drain, 0)
    for wait in waits:
        wait[1].wait()
    second_hop = []
    for k, copy in zip((1, 3, 2), (first_hop[1], first_hop[2], first_hop[0])):
        copy.wait_recv()
        second_hop.append(gather(4 + k, in_time[4 - k], other))
        second_hop[-1].start()
    first_hop[3].wait_recv()
    for copy in second_hop:
        copy.wait_recv()
    coarse_ref[...] = posted[...].astype(F32)
    for copy in first_hop + second_hop:
        copy.wait_send()
    put_x.wait()


def hand_over(x_in, coarse_in, x_out, coarse_out):
    x_out[...] = x_in[...]
    coarse_out[...] = coarse_in[...]


def per_device(right_side, hop_blocks, restriction):
    right = jnp.transpose(right_side[0], (1, 0, 2)).reshape(ROWS, 128)
    shapes = (jax.ShapeDtypeStruct((ROWS, 128), F32), jax.ShapeDtypeStruct((8, 4 * RHS, 128), F32))
    held = pl.pallas_call(
        body,
        out_shape=shapes,
        in_specs=[pl.BlockSpec(memory_space=pl.ANY)] * 3,
        out_specs=(pl.BlockSpec(memory_space=pl.ANY), pl.BlockSpec(memory_space=pltpu.VMEM)),
        scratch_shapes=[
            pltpu.VMEM((ROWS, 128), F32),
            pltpu.VMEM((SITES, 9, 64, 128), BF16),
            pltpu.VMEM((SITES, 64, 128), F32),
            pltpu.VMEM((ITERS + 1, ROWS, 128), F32),
            pltpu.VMEM((ITERS, 2, 2, SLAB, 128), BF16),
            pltpu.VMEM((2, 2, 2, SLAB, 128), BF16),
            pltpu.VMEM((ITERS, 4, 2, 2, SLAB, 128), BF16),
            pltpu.VMEM((ITERS, 2, 2, SLAB, 128), BF16),
            pltpu.VMEM((4, 192, 256), F32),
            pltpu.VMEM((24, 128), F32),
            pltpu.VMEM((5, 4, 128), F32),
            pltpu.VMEM((3, 4, 128), F32),
            pltpu.VMEM((16, 4, 128), F32),
            pltpu.VMEM((8, 4, 128), F32),
            pltpu.VMEM((8, 128), F32),
            pltpu.VMEM((ITERS + 1, PACK, 128), F32),
            pltpu.VMEM((SITES, 64, 128), BF16),
            pltpu.VMEM((SITES, 64, 128), BF16),
            pltpu.VMEM((4 * RHS, 128), F32),
            pltpu.VMEM((8, 4 * RHS, 128), BF16),
            pltpu.VMEM((ROWS, 128), F32),
            pltpu.SemaphoreType.DMA((3,)),
            pltpu.SemaphoreType.DMA((ITERS, 6)),
            pltpu.SemaphoreType.DMA((ITERS, 6)),
            pltpu.SemaphoreType.DMA((5,)),
            pltpu.SemaphoreType.DMA((5,)),
            pltpu.SemaphoreType.DMA((8,)),
            pltpu.SemaphoreType.DMA((8,)),
            pltpu.SemaphoreType.DMA((1,)),
        ],
        compiler_params=pltpu.CompilerParams(
            collective_id=0, has_side_effects=True, vmem_limit_bytes=56 * 1024 * 1024
        ),
        cost_estimate=pl.CostEstimate(flops=500_000_000, bytes_accessed=4_000_000, transcendentals=0),
        name="smooth",
    )(right, hop_blocks[0], restriction[0])
    x, coarse = pl.pallas_call(
        hand_over,
        out_shape=shapes,
        in_specs=[pl.BlockSpec(memory_space=pltpu.VMEM)] * 2,
        out_specs=(pl.BlockSpec(memory_space=pltpu.VMEM),) * 2,
        name="hand_over",
    )(*held)
    x = jnp.transpose(x.reshape(RHS, SITES, 128), (1, 0, 2))[None]
    return x, jnp.transpose(coarse.reshape(8, RHS, 4, 128), (0, 2, 1, 3))


def solution(mesh):
    placed = (
        P("narrow", "wide", None, None),
        P("narrow", "wide", None, None, None),
        P("narrow", "wide", None, None),
    )
    return jax.shard_map(
        per_device,
        mesh=mesh,
        in_specs=placed,
        out_specs=(P("narrow", "wide", None, None), P(None, "wide", None, None)),
        check_vma=False,
    )
```

```python
import jax
import jax.numpy as jnp
from jax import lax
from jax.experimental import pallas as pl
from jax.experimental.pallas import tpu as pltpu
from jax.sharding import PartitionSpec as P

F32, BF16 = jnp.float32, jnp.bfloat16
MESH = pl.DeviceIdType.MESH
ITERS = 4
RHS = 12
SITES = 16
HALF = 64
ROWS = SITES * RHS
SLAB = ROWS // 2
PACK = 4 * RHS
SCALE = 1.0 / 16.0


def dot(lhs, rhs):
    return lax.dot_general(lhs, rhs, (((1,), (1,)), ((), ())), preferred_element_type=F32)


def mod(value, size):
    return lax.rem(value, jnp.int32(size))


def div(value, size):
    return lax.div(value, jnp.int32(size))


def split(value):
    high = value.astype(BF16)
    return high, (value - high.astype(F32)).astype(BF16)


def paired(rows):
    lane = lax.broadcasted_iota(jnp.int32, rows.shape, 1)
    sign = jnp.where(lane < HALF, 1.0, -1.0).astype(rows.dtype)
    return jnp.concatenate([rows * sign, pltpu.roll(rows, HALF, 1)], 0)


def unpack(first, second):
    first = jnp.concatenate([first[0:24, 0:128], first[24:48, 128:256]], 0)
    second = jnp.concatenate([second[0:24, 0:128], second[24:48, 128:256]], 0)
    row = lax.broadcasted_iota(jnp.int32, (PACK, 128), 0)
    lane = lax.broadcasted_iota(jnp.int32, (PACK, 128), 1)
    even = (row < 12) | ((row >= 24) & (row < 36))
    moved = pltpu.roll(jnp.where(even, second, first), HALF, 1)
    return jnp.where(even == (lane < HALF), jnp.where(even, first, second), moved)


def body(
    right_ref, hop_ref, rest_ref, x_ref, posted,
    rin, hop, rest, vecs, sent, local, big, rows, acc, grams, message, slots0, slots1, slots2, wide_msg,
    coarse, rest_hi, rest_lo, mine, xout,
    load_sem, send_sem, recv_sem, red_send, red_recv, gat_send, gat_recv, out_sem,
):
    w = lax.axis_index("wide")
    n = lax.axis_index("narrow")
    px, zlat = mod(w, 8), div(w, 8)
    pz, plo = mod(zlat, 8), div(w, 64)
    phi, pc = div(n, 2), mod(n, 2)

    load_right = pltpu.make_async_copy(right_ref, rin, load_sem.at[0])
    load_right.start()
    load_hop = pltpu.make_async_copy(hop_ref, hop, load_sem.at[1])
    load_hop.start()
    load_rest = pltpu.make_async_copy(rest_ref, rest, load_sem.at[2])
    load_rest.start()

    in_x = [zlat * 8 + mod(px + d, 8) for d in range(8)]
    in_z = [mod(pz + d, 8) * 8 + px for d in range(8)]
    in_time = [mod(phi + d, 4) * 2 + pc for d in range(4)]

    z_up, z_down = (mod(zlat + 1, 16) * 8 + px, n), (mod(zlat + 15, 16) * 8 + px, n)
    y_up, y_down = (in_x[1], n), (in_x[7], n)
    t_up, t_down = (w, mod(n + 1, 8)), (w, mod(n + 7, 8))
    other = (w, n + 1 - 2 * pc)

    ahead = [mod(phi + 2 * pc, 4) * 2 + pc, mod(phi + 2 * pc + 1, 4) * 2 + pc]
    behind = [mod(phi + 4 - 2 * pc, 4) * 2 + pc, mod(phi + 3 - 2 * pc, 4) * 2 + pc]
    wide_to = [(w, in_time[2])] + [(in_x[k % 8], ahead[k // 8]) for k in range(1, 16)]
    wide_from = [(w, in_time[2])] + [(in_x[(8 - k) % 8], behind[k // 8]) for k in range(1, 16)]
    half = mod(plo + pc, 2) * 64
    deep_to = [(in_z[0] + 64 - 64 * plo, n)] + [(in_z[k] + half, n) for k in range(1, 8)]
    deep_from = [deep_to[0]] + [(in_z[8 - k] + half, n) for k in range(1, 8)]

    gathered = [(w, in_time[k]) for k in (2, 1, 3)]
    greeted = [z_up, z_down, t_up, t_down, y_up, y_down, (w, mod(phi + 1 + 2 * pc, 4) * 2 + pc)]
    greeted += wide_from + deep_from
    barrier = pltpu.get_barrier_semaphore()
    for device in greeted:
        pl.semaphore_signal(barrier, inc=1, device_id=device, device_id_type=MESH)

    load_right.wait()
    for site in range(SITES):
        vecs[0, pl.ds(RHS * site, RHS), :] = rin[pl.ds(site, RHS, stride=SITES), :]

    def outgoing(i):
        for y in range(2):
            sent[i, y, 0], sent[i, y, 1] = split(vecs[i, pl.ds(SLAB * y, SLAB), :])

    def shifted(i):
        for y in range(2):
            value = vecs[i, pl.ds(SLAB * y, SLAB), :]
            for at, shift in ((0, SLAB - RHS), (1, RHS)):
                local[at, y, 0], local[at, y, 1] = split(pltpu.roll(value, shift, 0))

    def halo(i):
        plans = [
            (sent.at[i], big.at[i, 0], z_down),
            (sent.at[i], big.at[i, 1], z_up),
            (sent.at[i], big.at[i, 2], t_down),
            (sent.at[i], big.at[i, 3], t_up),
            (sent.at[i, 0], rows.at[i, 1], y_down),
            (sent.at[i, 1], rows.at[i, 0], y_up),
        ]
        return [
            pltpu.make_async_remote_copy(
                src_ref=src, dst_ref=dst, send_sem=send_sem.at[i, k], recv_sem=recv_sem.at[i, k],
                device_id=device, device_id_type=MESH,
            )
            for k, (src, dst, device) in enumerate(plans)
        ]

    def gram(i):
        lane = lax.broadcasted_iota(jnp.int32, (24, 128), 1)
        sign = jnp.where(lane < HALF, -1.0, 1.0)[None]
        left = vecs[i].reshape(8, 24, 128)
        turned = pltpu.roll(vecs[i], HALF, 1).reshape(8, 24, 128) * sign

        def one(j, total):
            right = vecs[j].reshape(8, 24, 128)
            real = jnp.sum(jnp.sum(left * right, 0), 1, keepdims=True)
            imag = jnp.sum(jnp.sum(turned * right, 0), 1, keepdims=True)
            entry = i * (i + 1) // 2 + j
            return total + jnp.where(lane == entry, real, 0.0) + jnp.where(lane == entry + 16, imag, 0.0)

        if isinstance(i, int):
            total = grams[...]
            for j in range(i + 1):
                total = one(j, total)
            return total
        grams[...] = lax.fori_loop(0, i + 1, one, grams[...])

    def weights(y, h, directions):
        first = 8 * y + 4 * h
        return jnp.concatenate([hop[pl.ds(first, 4), d].reshape(256, 128) for d in directions], 1)

    def fields(views, h):
        at = pl.ds(PACK * h, PACK)
        return jnp.concatenate([paired(jnp.concatenate([v[0, at, :], v[1, at, :]], 0)) for v in views], 1)

    groups = [(y, h) for y in range(2) for h in range(2)]

    def early(i):
        for g, (y, h) in enumerate(groups):
            views = [sent.at[i, y], local.at[0, y], local.at[1, y], sent.at[i, 1 - y]]
            acc[g] = dot(fields(views, h), weights(y, h, [0, 1, 2, 3 + y]))

    def middle(i):
        for g, (y, h) in enumerate(groups):
            views = [rows.at[i, y], big.at[i, 0, y], big.at[i, 1, y]]
            acc[g] += dot(fields(views, h), weights(y, h, [4 - y, 5, 6]))

    def late(i):
        for g, (y, h) in enumerate(groups):
            views = [big.at[i, 2, y], big.at[i, 3, y]]
            total = acc[g] + dot(fields(views, h), weights(y, h, [7, 8]))
            first = total[0:48] + total[48:96]
            second = total[96:144] + total[144:192]
            vecs[i + 1, pl.ds(SLAB * y + PACK * h, PACK), :] = unpack(first, second) * SCALE

    grams[...] = jnp.zeros((24, 128), F32)
    outgoing(0)
    pl.semaphore_wait(barrier, len(greeted))

    def iteration(i, carry):
        copies = halo(i)
        for copy in copies:
            copy.start()
        shifted(i)

        @pl.when(i == 0)
        def _():
            load_hop.wait()

        @pl.when(i == 1)
        def _():
            load_rest.wait()
            for site in range(SITES):
                rest_hi[site], rest_lo[site] = split(rest[site])

        early(i)
        gram(i)
        for k in (4, 5, 0, 1):
            copies[k].wait_recv()
        middle(i)
        for k in (2, 3):
            copies[k].wait_recv()
        late(i)

        @pl.when(i < ITERS - 1)
        def _():
            outgoing(i + 1)

        return carry

    lax.fori_loop(0, ITERS, iteration, 0)
    sums = gram(ITERS)

    both = sums + pltpu.roll(sums, RHS, 0)
    packed = both[0:8] + pltpu.roll(both[8:16], 32, 1) + pltpu.roll(both[16:24], 64, 1)
    message[0] = packed[0:4]

    def reduce_over(phase, partners, slots):
        copies = [
            pltpu.make_async_remote_copy(
                src_ref=message.at[phase], dst_ref=slots.at[k],
                send_sem=red_send.at[phase], recv_sem=red_recv.at[phase],
                device_id=device, device_id_type=MESH,
            )
            for k, device in enumerate(partners)
        ]
        for copy in copies:
            copy.start()
        return [pltpu.make_async_copy(slots, slots, sem.at[phase]) for sem in (red_recv, red_send)]

    def part(own, slots):
        return jnp.sum(slots[1:], 0) + jnp.where(pc == 0, own, slots[0])

    def restrict(j):
        pieces = []
        for h in range(2):
            rows_of = [split(vecs[j, pl.ds(SLAB * y + PACK * h, PACK), :]) for y in range(2)]
            both_rows = jnp.concatenate([paired(jnp.concatenate(p, 0)) for p in rows_of], 1)
            high_rows = jnp.concatenate([paired(p[0]) for p in rows_of], 1)

            def blocks(ref):
                return jnp.concatenate([ref[8 * y + 4 * h : 8 * y + 4 * h + 4].reshape(256, 128) for y in range(2)], 1)

            main = dot(both_rows, blocks(rest_hi))
            remainder = dot(high_rows, blocks(rest_lo))
            first = main[0:48] + main[48:96] + remainder[0:48]
            second = main[96:144] + main[144:192] + remainder[48:96]
            value = unpack(first, second)
            value = value + pltpu.roll(value, PACK - RHS, 0)
            pieces += [value[0:12], value[24:36]]
        coarse[j] = jnp.concatenate(pieces, 0)

    def restrict_some(start, stop):
        def one(j, carry):
            restrict(j)
            return carry

        lax.fori_loop(start, stop, one, 0)

    waits = [reduce_over(0, [other], slots0.at[0:1])]
    waits[0][0].wait()
    message[1] = message[0] + slots0[0]
    waits.append(reduce_over(1, wide_to, slots1))
    restrict_some(0, 3)
    waits[1][0].wait()
    message[2] = part(message[1], slots1[...])
    waits.append(reduce_over(2, [other], slots0.at[1:2]))
    waits[2][0].wait()
    message[3] = message[2] + slots0[1]
    waits.append(reduce_over(3, deep_to, slots2))

    def drain(i, carry):
        for copy in halo(i):
            copy.wait_send()
        return carry

    restrict_some(3, 5)
    waits[3][0].wait()
    message[4] = part(message[3], slots2[...])
    waits.append(reduce_over(4, [other], slots0.at[2:3]))
    waits[4][0].wait()
    total = message[4] + slots0[2]
    wide_msg[0:4, :] = total
    wide_msg[4:8, :] = total
    table = wide_msg[...]

    def entry(e):
        return pltpu.roll(table, (128 - e) % 128, 1)

    g = {}
    for i in range(5):
        for j in range(i + 1):
            e = i * (i + 1) // 2 + j
            g[i, j] = (entry(e), entry(16 + e) if i != j else jnp.zeros((8, 128), F32))

    def times(a, b):
        return a[0] * b[0] - a[1] * b[1], a[0] * b[1] + a[1] * b[0]

    def minus(a, b):
        return a[0] - b[0], a[1] - b[1]

    alphas = []
    for k in range(ITERS):
        inner, power = g[1, 0], g[1, 1][0]
        alpha = (inner[0] / power, inner[1] / power)
        alphas.append(alpha)
        size = alpha[0] * alpha[0] + alpha[1] * alpha[1]
        if k == ITERS - 1:
            break
        top = 4 - k
        later = {}
        for i in range(1, top):
            for j in range(i + 1):
                ahead = g[i, j + 1] if j + 1 <= i else (g[j + 1, i][0], -g[j + 1, i][1])
                value = minus(g[i, j], times(alpha, ahead))
                value = minus(value, times((alpha[0], -alpha[1]), g[i + 1, j]))
                far = g[i + 1, j + 1]
                later[i, j] = (value[0] + size * far[0], value[1] + size * far[1])
        g = later

    one = (jnp.ones((8, 128), F32), jnp.zeros((8, 128), F32))
    residual = [one]
    iterate = []
    for alpha in alphas:
        scaled = (alpha[0] * SCALE, alpha[1] * SCALE)
        added = [times(scaled, c) for c in residual]
        iterate = [
            (a[0] + b[0], a[1] + b[1]) if b is not None else a
            for a, b in zip(added, iterate + [None] * (len(added) - len(iterate)))
        ]
        moved = [times(alpha, c) for c in residual]
        grown = [residual[0]]
        for j in range(1, len(residual)):
            grown.append(minus(residual[j], moved[j - 1]))
        grown.append((-moved[-1][0], -moved[-1][1]))
        residual = grown

    sub = lax.broadcasted_iota(jnp.int32, (8, 128), 0) < 4
    left_half = lax.broadcasted_iota(jnp.int32, (24, 128), 1) < HALF

    def spread(value):
        c0, c1, c2 = (jnp.broadcast_to(value[:, at : at + 1], (8, 128)) for at in (0, 32, 64))
        return jnp.concatenate([jnp.where(sub, c0, c2), jnp.where(sub, c1, c0), jnp.where(sub, c2, c1)], 0)

    def coefficient(pair):
        imag = spread(pair[1])
        return spread(pair[0])[None], jnp.where(left_half, -imag, imag)[None]

    last = coarse[0].reshape(2, 24, 128)
    for j in range(1, 5):
        re, im = coefficient(residual[j])
        last = last + re * coarse[j].reshape(2, 24, 128)
        last = last + im * pltpu.roll(coarse[j], HALF, 1).reshape(2, 24, 128)
    last = last.reshape(PACK, 128)
    for at in range(4):
        mine[pl.ds(at, RHS, stride=4), :] = last[RHS * at : RHS * (at + 1)]
    posted[n] = mine[...].astype(BF16)

    def gather(k, slot, device):
        return pltpu.make_async_remote_copy(
            src_ref=posted.at[slot], dst_ref=posted.at[slot], send_sem=gat_send.at[k], recv_sem=gat_recv.at[k],
            device_id=device, device_id_type=MESH,
        )

    first_hop = [gather(k, n, device) for k, device in zip((2, 1, 3), gathered)]
    first_hop.append(gather(0, n, other))
    for copy in first_hop:
        copy.start()
    field = jnp.zeros((8, 24, 128), F32)
    for j in range(ITERS):
        re, im = coefficient(iterate[j])
        field = field + re * vecs[j].reshape(8, 24, 128)
        field = field + im * pltpu.roll(vecs[j], HALF, 1).reshape(8, 24, 128)
    field = field.reshape(ROWS, 128)
    for site in range(SITES):
        xout[pl.ds(site, RHS, stride=SITES), :] = field[RHS * site : RHS * (site + 1)]
    put_x = pltpu.make_async_copy(xout, x_ref, out_sem.at[0])
    put_x.start()
    lax.fori_loop(0, ITERS, drain, 0)
    for wait in waits:
        wait[1].wait()
    second_hop = []
    for k, copy in zip((1, 3, 2), (first_hop[1], first_hop[2], first_hop[0])):
        copy.wait_recv()
        second_hop.append(gather(4 + k, in_time[4 - k], other))
        second_hop[-1].start()
    first_hop[3].wait_recv()
    for copy in second_hop:
        copy.wait_recv()
    for copy in first_hop + second_hop:
        copy.wait_send()
    put_x.wait()


def hand_over(x_in, coarse_in, x_out, coarse_out):
    x_out[...] = x_in[...]
    coarse_out[...] = coarse_in[...].astype(F32)


def per_device(right_side, hop_blocks, restriction):
    right = jnp.transpose(right_side[0], (1, 0, 2)).reshape(ROWS, 128)
    def shapes(kind):
        return (jax.ShapeDtypeStruct((ROWS, 128), F32), jax.ShapeDtypeStruct((8, 4 * RHS, 128), kind))

    held = pl.pallas_call(
        body,
        out_shape=shapes(BF16),
        in_specs=[pl.BlockSpec(memory_space=pl.ANY)] * 3,
        out_specs=(pl.BlockSpec(memory_space=pl.ANY), pl.BlockSpec(memory_space=pltpu.VMEM)),
        scratch_shapes=[
            pltpu.VMEM((ROWS, 128), F32),
            pltpu.VMEM((SITES, 9, 64, 128), BF16),
            pltpu.VMEM((SITES, 64, 128), F32),
            pltpu.VMEM((ITERS + 1, ROWS, 128), F32),
            pltpu.VMEM((ITERS, 2, 2, SLAB, 128), BF16),
            pltpu.VMEM((2, 2, 2, SLAB, 128), BF16),
            pltpu.VMEM((ITERS, 4, 2, 2, SLAB, 128), BF16),
            pltpu.VMEM((ITERS, 2, 2, SLAB, 128), BF16),
            pltpu.VMEM((4, 192, 256), F32),
            pltpu.VMEM((24, 128), F32),
            pltpu.VMEM((5, 4, 128), F32),
            pltpu.VMEM((3, 4, 128), F32),
            pltpu.VMEM((16, 4, 128), F32),
            pltpu.VMEM((8, 4, 128), F32),
            pltpu.VMEM((8, 128), F32),
            pltpu.VMEM((ITERS + 1, PACK, 128), F32),
            pltpu.VMEM((SITES, 64, 128), BF16),
            pltpu.VMEM((SITES, 64, 128), BF16),
            pltpu.VMEM((4 * RHS, 128), F32),
            pltpu.VMEM((ROWS, 128), F32),
            pltpu.SemaphoreType.DMA((3,)),
            pltpu.SemaphoreType.DMA((ITERS, 6)),
            pltpu.SemaphoreType.DMA((ITERS, 6)),
            pltpu.SemaphoreType.DMA((5,)),
            pltpu.SemaphoreType.DMA((5,)),
            pltpu.SemaphoreType.DMA((8,)),
            pltpu.SemaphoreType.DMA((8,)),
            pltpu.SemaphoreType.DMA((1,)),
        ],
        compiler_params=pltpu.CompilerParams(
            collective_id=0, has_side_effects=True, vmem_limit_bytes=56 * 1024 * 1024
        ),
        cost_estimate=pl.CostEstimate(flops=500_000_000, bytes_accessed=4_000_000, transcendentals=0),
        name="smooth",
    )(right, hop_blocks[0], restriction[0])
    x, coarse = pl.pallas_call(
        hand_over,
        out_shape=shapes(F32),
        in_specs=[pl.BlockSpec(memory_space=pltpu.VMEM)] * 2,
        out_specs=(pl.BlockSpec(memory_space=pltpu.VMEM),) * 2,
        name="hand_over",
    )(*held)
    x = jnp.transpose(x.reshape(RHS, SITES, 128), (1, 0, 2))[None]
    return x, jnp.transpose(coarse.reshape(8, RHS, 4, 128), (0, 2, 1, 3))


def solution(mesh):
    placed = (
        P("narrow", "wide", None, None),
        P("narrow", "wide", None, None, None),
        P("narrow", "wide", None, None),
    )
    return jax.shard_map(
        per_device,
        mesh=mesh,
        in_specs=placed,
        out_specs=(P("narrow", "wide", None, None), P(None, "wide", None, None)),
        check_vma=False,
    )
```
